256 devices in a mesh: ctx: 64 (over x_hi, y, z), tp: 4 (over x_lo, core).
Axes of the slice: x: 4 (x_hi: 2, x_lo: 2; x = x_hi * 2 + x_lo), y: 4, z: 8, core: 2. Of those that a mesh axis runs over, the one named last changes fastest.
Arguments:
- queries: bfloat16 [16384, 4096], P('ctx', 'tp'), may hold values from -6 to 6
- keys: bfloat16 [16384, 512], P('ctx', 'tp'), may hold values from -6 to 6
- values: bfloat16 [16384, 512], P('ctx', 'tp'), may hold values from -6 to 6
- outputs: bfloat16 [16384, 4096], P('ctx', 'tp'), may hold values from -4 to 4
- grad_out: bfloat16 [16384, 4096], P('ctx', 'tp'), may hold values from -4 to 4
- log_sums: float32 [32, 16384], P('tp', 'ctx'), may hold values from 1.5 to 3.5
- block_mask: int32 [64, 3], P('ctx'), may hold values from 0 to 1, as said below
- grad_tokens: bfloat16 [16384, 4096], P('ctx', 'tp'), may hold values from -6 to 6
- expert_ids: int32 [16384, 2], P('ctx'), may hold values from 0 to 63, all different within a row; in each aligned block of 256 rows (0 to 255, 256 to 511, ...) at most 16 rows name the same one
- route_probs: float32 [16384, 2], P('ctx'), may hold values from 0.05 to 0.6
- hidden_saved: bfloat16 [64, 1024, 1536], P('ctx', None, 'tp'), may hold values from -6 to 6
- down_weight: bfloat16 [64, 1536, 4096], P('ctx', None, 'tp'), may hold values from -0.15625 to 0.15625
Outputs:
- grad_queries: bfloat16 [16384, 4096], P('ctx', 'tp')
- grad_keys: bfloat16 [16384, 512], P('ctx', 'tp')
- grad_values: bfloat16 [16384, 512], P('ctx', 'tp')
- grad_weight: bfloat16 [64, 1536, 4096], P('ctx', None, 'tp')
- grad_hidden: bfloat16 [64, 1536, 1024], P('ctx', 'tp')
The draws below stay inside these ranges and needn't reach their ends.
Inputs may be any that keep to these rules, and one draw needn't show every extreme that they name: `expert_ids`: among the routes of one block of 256 tokens, no expert is named more than 16 times, a bound that some block reaches; a token names 2 different experts. block_mask[r, r - 1] = 1 for r = 1 .. 3: block r attends the first block.
All inputs are finite; a program needn't handle non-finite values.
Results may differ from the reference program's by a relative error of at most 0.0052.
Values may be sent and summed in bfloat16 or wider, within the bound.
A program may use at most 128 MiB of HBM per device.

```python
import math
import jax
import jax.numpy as jnp
import numpy as np
from jax import lax

D = 4096
FF = 1536
HEADS = 32
KVH = 4
HD = 128
TOK = 256
WIN = 4
TOPW = 2
EXPERTS = 64
TOKENS = 16384
CAP = 16
SLOTS = 1024
N_CTX = 64


def draw_block_mask(key, part):
    key = jax.random.fold_in(key, 7)
    drawn = (jax.random.randint(key, (N_CTX, WIN - 1), 0, 4) < 3).astype(jnp.int32)
    row_index = jnp.arange(N_CTX, dtype=jnp.int32)[:, None]
    lag_column = jnp.arange(WIN - 1, dtype=jnp.int32)[None, :]
    return jnp.where(row_index == lag_column + 1, 1, drawn).astype(jnp.int32)


def shard_levels(key, dims, shards, low, largest):
    factor_of, own = 1.0, jax.random.fold_in(key, 6)
    for dim, blocks in shards:
        steps = jnp.exp(jax.random.uniform(jax.random.fold_in(own, dim), (blocks,), jnp.float32, low / len(shards), largest / len(shards)))
        factor_of = factor_of * jnp.repeat(steps, dims[dim] // blocks).reshape([-1 if axis == dim else 1 for axis in range(len(dims))])
    return factor_of


def routed_block(stream_key, own, number, rows, count, top, limit, lean):
    order = jax.random.permutation(stream_key, count)
    packed, ordinary = portions_of(count, rows * top, limit, lean, True), portions_of(count, rows * top, limit, lean, False)
    places = jnp.arange(count)

    def named(tallies, rotation):
        used = int((tallies > 0).sum())
        fixed = max(1, used // 4)
        moved = fixed + (places - fixed + rotation * (used - fixed)) % max(1, count - fixed)
        return jnp.zeros((count,), jnp.int32).at[order[jnp.where(places < fixed, places, moved)]].set(jnp.asarray(tallies, jnp.int32))

    tallies = jnp.where(number % 4 == 0, named(packed, number // 4), named(ordinary, number - number // 4 - 1))
    mixed = jax.random.permutation(jax.random.fold_in(own, 3), count)
    giver, taker = mixed[0:count // 2 * 2:2], mixed[1:count // 2 * 2:2]
    slack = jnp.minimum(tallies[giver] - 1, limit - tallies[taker]) // 2
    slack = jnp.where((giver == order[0]) | (taker == order[0]) | (tallies[taker] == 0), 0, jnp.maximum(slack, 0))
    moved = jax.random.randint(jax.random.fold_in(own, 4), (count // 2,), 0, 1 << 20) % (slack + 1)
    tallies = tallies.at[giver].add(-moved).at[taker].add(moved)
    members = jnp.searchsorted(jnp.cumsum(tallies), jnp.arange(rows * top), side="right").astype(jnp.int32)
    table = members.reshape(top, rows).T
    table = table[jax.random.permutation(jax.random.fold_in(own, 1), rows)]
    rotation = jax.random.randint(jax.random.fold_in(own, 2), (rows, 1), 0, top)
    return jnp.take_along_axis(table, (jnp.arange(top)[None, :] + rotation) % top, axis=1)


def portions_of(amount, total, most, slope, full):
    portions = [(1 << 20) // math.isqrt(grade ** slope) + 1 for grade in range(1, amount + 1)]
    largest = most if full else min(most, max(-(-total // amount), total * portions[0] // sum(portions)))
    least = 1 if total - largest >= amount - 1 else 0
    holding, rest = [largest] + [least] * (amount - 1), total - largest - least * (amount - 1)
    while rest > 0:
        movable = [i for i in range(1, amount) if holding[i] < largest] or [i for i in range(1, amount) if holding[i] < most]
        pool, left = sum([portions[i] for i in movable]), rest
        for i in movable:
            more = min(most - holding[i], max(1, left * portions[i] // pool), rest)
            holding[i] = holding[i] + more
            rest = rest - more
    return np.array(holding)


def centred(stream_key, extent, scale, most, split=(), held_as=jnp.bfloat16):
    values = jax.random.normal(stream_key, extent, jnp.float32) * scale
    if len(split) > 0:
        values = shard_levels(stream_key, extent, split, -0.22, 0.18) * values
    return jnp.clip(values, min=-most, max=most).astype(held_as)


def setup_inputs(seed: int = 0) -> dict:
    arg_keys = jax.random.split(jax.random.key(seed), 13)
    queries = centred(arg_keys[0], (TOKENS, HEADS * HD), 1.0, 6.0, ((0, 64), (1, 4)))
    keys = centred(arg_keys[1], (TOKENS, KVH * HD), 1.0, 6.0, ((0, 64), (1, 4)))
    values = centred(arg_keys[2], (TOKENS, KVH * HD), 1.0, 6.0, ((0, 64), (1, 4)))
    outputs = centred(arg_keys[3], (TOKENS, HEADS * HD), 0.3, 4.0, ((0, 64), (1, 4)))
    grad_out = centred(arg_keys[4], (TOKENS, HEADS * HD), 0.3, 4.0, ((0, 64), (1, 4)))
    log_sums = jnp.clip(1.5 + 2.0 * jax.random.uniform(arg_keys[5], (HEADS, TOKENS), jnp.float32) ** shard_levels(arg_keys[5], (HEADS, TOKENS), ((0, 4), (1, 64)), -0.2, 0.2), 1.5, 3.5)
    block_mask = draw_block_mask(jax.random.fold_in(arg_keys[12], 71), 0)
    grad_tokens = centred(arg_keys[7], (TOKENS, D), 1.0, 6.0, ((0, 64), (1, 4)))
    expert_ids_keys = jax.random.split(jax.random.fold_in(arg_keys[8], 1), TOKENS // TOK)
    expert_ids_turns = jax.random.permutation(jax.random.fold_in(arg_keys[8], 3), TOKENS // TOK)
    expert_ids = jax.vmap(lambda own, number: routed_block(jax.random.fold_in(arg_keys[8], 2), own, number, TOK, EXPERTS, TOPW, CAP, 2))(expert_ids_keys, expert_ids_turns).reshape((TOKENS, TOPW))
    route_probs = jnp.clip(0.05 + 0.55 * jax.random.uniform(arg_keys[9], (TOKENS, TOPW), jnp.float32) ** shard_levels(arg_keys[9], (TOKENS, TOPW), ((0, 64),), -0.2, 0.2), 0.05, 0.6)
    hidden_saved = centred(arg_keys[10], (EXPERTS, SLOTS, FF), 1.0, 6.0, ((0, 64), (2, 4)))
    down_weight = centred(arg_keys[11], (EXPERTS, FF, D), FF ** -0.5, 0.15625, ((0, 64), (2, 4)))
    return {"queries": queries, "keys": keys, "values": values, "outputs": outputs, "grad_out": grad_out, "log_sums": log_sums, "block_mask": block_mask, "grad_tokens": grad_tokens, "expert_ids": expert_ids, "route_probs": route_probs, "hidden_saved": hidden_saved, "down_weight": down_weight}


def round_low(array):
    return lax.optimization_barrier(array.astype(jnp.bfloat16)).astype(jnp.float32)


def query_block(operands):
    query_heads, grad_heads, delta_rows, log_heads, key_stack, value_stack, live_flags = operands
    score_scale = HD ** -0.5
    causal = jnp.tril(jnp.ones((TOK, TOK), jnp.float32))
    grad_query = jnp.zeros(query_heads.shape, jnp.float32)
    key_parts = []
    value_parts = []
    for lag_index in range(WIN):
        key_block = key_stack[lag_index]
        value_block = value_stack[lag_index]
        scores = jnp.einsum('tkgd,ukd->kgtu', query_heads, key_block) * score_scale
        weights = jnp.exp(scores - log_heads[..., None])
        if lag_index == 0:
            weights = weights * causal
        else:
            weights = weights * live_flags[lag_index - 1]
        weights_low = round_low(weights)
        value_parts.append(jnp.einsum('kgtu,tkgd->ukd', weights_low, grad_heads))
        grad_weights = jnp.einsum('tkgd,ukd->kgtu', grad_heads, value_block)
        grad_scores = round_low(weights * (grad_weights - delta_rows[..., None]))
        grad_query = grad_query + jnp.einsum('kgtu,ukd->tkgd', grad_scores, key_block) * score_scale
        key_parts.append(jnp.einsum('kgtu,tkgd->ukd', grad_scores, query_heads) * score_scale)
    return grad_query, jnp.stack(key_parts), jnp.stack(value_parts)


def reference(queries, keys, values, outputs, grad_out, log_sums, block_mask, grad_tokens, expert_ids, route_probs, hidden_saved, down_weight):
    blocks = N_CTX
    groups = HEADS // KVH
    query_all = queries.astype(jnp.float32).reshape(blocks, TOK, KVH, groups, HD)
    grad_all = grad_out.astype(jnp.float32).reshape(blocks, TOK, KVH, groups, HD)
    output_all = outputs.astype(jnp.float32).reshape(blocks, TOK, KVH, groups, HD)
    delta_all = jnp.sum(grad_all * output_all, axis=-1).transpose(0, 2, 3, 1)
    log_all = log_sums.reshape(KVH, groups, blocks, TOK).transpose(2, 0, 1, 3)
    key_all = keys.astype(jnp.float32).reshape(blocks, TOK, KVH, HD)
    value_all = values.astype(jnp.float32).reshape(blocks, TOK, KVH, HD)
    key_stack = jnp.stack([jnp.roll(key_all, lag_index, axis=0) for lag_index in range(WIN)], axis=1)
    value_stack = jnp.stack([jnp.roll(value_all, lag_index, axis=0) for lag_index in range(WIN)], axis=1)
    position = jnp.arange(blocks, dtype=jnp.int32)
    live_all = jnp.stack([((position - lag_index) >= 0) & (block_mask[:, lag_index - 1] == 1) for lag_index in range(1, WIN)], axis=1).astype(jnp.float32)
    grad_query, key_parts, value_parts = lax.map(query_block, (query_all, grad_all, delta_all, log_all, key_stack, value_stack, live_all))
    grad_key = jnp.zeros((blocks, TOK, KVH, HD), jnp.float32)
    grad_value = jnp.zeros((blocks, TOK, KVH, HD), jnp.float32)
    for lag_index in range(WIN):
        grad_key = grad_key + jnp.roll(key_parts[:, lag_index], -lag_index, axis=0)
        grad_value = grad_value + jnp.roll(value_parts[:, lag_index], -lag_index, axis=0)
    grad_queries = grad_query.reshape(TOKENS, HEADS * HD).astype(jnp.bfloat16)
    grad_keys = grad_key.reshape(TOKENS, KVH * HD).astype(jnp.bfloat16)
    grad_values = grad_value.reshape(TOKENS, KVH * HD).astype(jnp.bfloat16)

    route_count = TOK * TOPW
    flat_ids = expert_ids.reshape(blocks, route_count)
    one_hot = (flat_ids[..., None] == jnp.arange(EXPERTS, dtype=jnp.int32)[None, None, :]).astype(jnp.int32)
    earlier = jnp.cumsum(one_hot, axis=1, dtype=jnp.int32) - one_hot
    slot_index = jnp.sum(earlier * one_hot, axis=2, dtype=jnp.int32)
    target = flat_ids * SLOTS + position[:, None] * CAP + slot_index
    source = jnp.zeros((EXPERTS * SLOTS,), jnp.int32).at[target.reshape(-1)].set(jnp.arange(blocks * route_count, dtype=jnp.int32) + 1).reshape(EXPERTS, SLOTS)
    flat_probs = route_probs.reshape(-1)

    def expert_grads(operands):
        picks, hidden_rows, weight_rows = operands
        chosen = jnp.maximum(picks - 1, 0)
        factor = jnp.where(picks > 0, flat_probs[chosen], 0.0)
        routed = (grad_tokens[chosen // TOPW].astype(jnp.float32) * factor[:, None]).astype(jnp.bfloat16)
        weight_grad = lax.dot_general(hidden_rows, routed, (((0,), (0,)), ((), ())), preferred_element_type=jnp.float32)
        hidden_grad = lax.dot_general(weight_rows, routed, (((1,), (1,)), ((), ())), preferred_element_type=jnp.float32)
        return weight_grad.astype(jnp.bfloat16), hidden_grad.astype(jnp.bfloat16)

    grad_weight, grad_hidden = lax.map(expert_grads, (source, hidden_saved, down_weight))
    return (grad_queries, grad_keys, grad_values, grad_weight, grad_hidden)
```

```python
import jax
import jax.numpy as jnp
from jax import lax
from jax.experimental import pallas as pl
from jax.experimental.pallas import tpu as pltpu
from jax.sharding import PartitionSpec as P

HD = 128
WIN = 4
CTX = 64
CAP = 16
MESH = pl.DeviceIdType.MESH


def shifted(x, axis, by):
    devices = lax.axis_size(axis)
    pairs = [(i, i + by) for i in range(devices) if 0 <= i + by < devices]
    return lax.ppermute(x, axis, pairs)


def passed_along(block, axis, distance):
    devices = range(lax.axis_size(axis))
    route = [((i - distance) % len(devices), i) for i in devices]
    return lax.ppermute(block, axis, route)


def place(ctx, offset):
    x = lax.rem(ctx // 32 + offset // 32, 2)
    y = lax.rem(lax.rem(ctx // 8, 4) + lax.rem(offset // 8, 4), 4)
    z = lax.rem(lax.rem(ctx, 8) + lax.rem(offset, 8), 8)
    return (x * 4 + y) * 8 + z


def exchange_kernel(tokens, ids, probs, received, routed, chosen, send_sem, recv_sems):
    ctx, tp = lax.axis_index("ctx"), lax.axis_index("tp")
    barrier = pltpu.get_barrier_semaphore()

    def greet(offset, carry):
        pl.semaphore_signal(barrier, inc=1, device_id=(place(ctx, offset), tp), device_id_type=MESH)
        return carry

    lax.fori_loop(1, CTX, greet, 0)

    count = tokens.shape[0]
    lanes = lax.broadcasted_iota(jnp.int32, (count, 128), 1)
    first, second = ids[:, 0:1] == lanes, ids[:, 1:2] == lanes
    both = (first | second).astype(jnp.bfloat16)
    below = (
        lax.broadcasted_iota(jnp.int32, (count, count), 0)
        > lax.broadcasted_iota(jnp.int32, (count, count), 1)
    ).astype(jnp.bfloat16)
    earlier = jnp.dot(below, both, preferred_element_type=jnp.float32)
    slots = []
    for rank, one_hot in enumerate((first, second)):
        slot = jnp.sum(jnp.where(one_hot, earlier, 0.0), axis=1, keepdims=True).astype(jnp.int32)
        slots.append(ids[:, rank : rank + 1] * CAP + slot)
        chosen[pl.ds(rank * count, count), :] = (
            tokens[...].astype(jnp.float32) * probs[:, rank : rank + 1]
        ).astype(jnp.bfloat16)

    def pick(column, carry):
        wanted = lanes + column * 128
        select = jnp.concatenate(
            [(slot == wanted).astype(jnp.bfloat16) for slot in slots], axis=0
        )
        routed[pl.ds(column * 128, 128), :] = lax.dot_general(
            select, chosen[...], (((0,), (0,)), ((), ())), preferred_element_type=jnp.float32
        ).astype(jnp.bfloat16)
        return carry

    lax.fori_loop(0, 8, pick, 0)
    pl.semaphore_wait(barrier, CTX - 1)

    def send(offset, carry):
        target = place(ctx, offset)
        pltpu.make_async_remote_copy(
            src_ref=routed.at[pl.ds(target * CAP, CAP)],
            dst_ref=received.at[pl.ds(ctx * CAP, CAP)],
            send_sem=send_sem,
            recv_sem=recv_sems.at[offset // 8],
            device_id=(target, tp),
            device_id_type=MESH,
        ).start()
        return carry

    lax.fori_loop(1, CTX, send, 0)
    received[pl.ds(ctx * CAP, CAP), :] = routed[pl.ds(ctx * CAP, CAP), :]
    for column in range(8):
        rows = pl.ds(0, 112 if column == 0 else 128)
        pltpu.make_async_copy(received.at[rows], received.at[rows], recv_sems.at[column]).wait()
    rows = pl.ds(0, (CTX - 1) * CAP)
    pltpu.make_async_copy(routed.at[rows], routed.at[rows], send_sem).wait()


def exchanged(tokens, ids, probs):
    width = tokens.shape[1]
    vmem = pl.BlockSpec(memory_space=pltpu.VMEM)
    return pl.pallas_call(
        exchange_kernel,
        out_shape=jax.ShapeDtypeStruct((CTX * CAP, width), jnp.bfloat16),
        in_specs=[vmem] * 3,
        out_specs=vmem,
        scratch_shapes=[
            pltpu.VMEM((CTX * CAP, width), jnp.bfloat16),
            pltpu.VMEM((2 * tokens.shape[0], width), jnp.bfloat16),
            pltpu.SemaphoreType.DMA,
            pltpu.SemaphoreType.DMA((8,)),
        ],
        compiler_params=pltpu.CompilerParams(
            collective_id=0, has_side_effects=True, vmem_limit_bytes=32 * 2**20
        ),
        name="exchange",
    )(tokens, ids, probs)


def shards(
    queries,
    keys,
    values,
    outputs,
    grad_out,
    log_sums,
    block_mask,
    grad_tokens,
    expert_ids,
    route_probs,
    hidden_saved,
    down_weight,
):
    tokens_here = queries.shape[0]
    kv_local = keys.shape[1] // HD
    groups = queries.shape[1] // HD // kv_local
    score_scale = HD ** (-0.5)
    query_heads = queries.reshape(tokens_here, kv_local, groups, HD)
    grad_heads = grad_out.reshape(tokens_here, kv_local, groups, HD)
    output_heads = outputs.reshape(tokens_here, kv_local, groups, HD)
    delta_rows = jnp.sum(
        grad_heads.astype(jnp.float32) * output_heads.astype(jnp.float32), axis=-1
    ).transpose(1, 2, 0)
    log_heads = log_sums.reshape(kv_local, groups, tokens_here)
    key_block = keys.reshape(tokens_here, kv_local, HD)
    value_block = values.reshape(tokens_here, kv_local, HD)
    position = lax.axis_index("ctx")
    causal = jnp.tril(jnp.ones((tokens_here, tokens_here), jnp.float32))

    def block_terms(key_rows, value_rows, live_flag):
        scores = (
            jnp.einsum("tkgd,ukd->kgtu", query_heads, key_rows, preferred_element_type=jnp.float32)
            * score_scale
        )
        weights = jnp.exp(scores - log_heads[..., None]) * live_flag
        weights_low = weights.astype(jnp.bfloat16)
        value_term = jnp.einsum(
            "kgtu,tkgd->ukd", weights_low, grad_heads, preferred_element_type=jnp.float32
        )
        grad_weights = jnp.einsum(
            "tkgd,ukd->kgtu", grad_heads, value_rows, preferred_element_type=jnp.float32
        )
        grad_scores = (weights * (grad_weights - delta_rows[..., None])).astype(jnp.bfloat16)
        query_term = (
            jnp.einsum("kgtu,ukd->tkgd", grad_scores, key_rows, preferred_element_type=jnp.float32)
            * score_scale
        )
        key_term = (
            jnp.einsum(
                "kgtu,tkgd->ukd", grad_scores, query_heads, preferred_element_type=jnp.float32
            )
            * score_scale
        )
        return (query_term, key_term, value_term)

    query_term, key_own, value_own = block_terms(key_block, value_block, causal)
    grad_query = query_term
    home_keys, home_values = (key_own, value_own)
    carried_keys, carried_values = (key_own, value_own)
    moving_keys, moving_values = (key_block, value_block)
    for lag_index in range(1, WIN):
        moving_keys, moving_values = shifted((moving_keys, moving_values), "ctx", 1)
        live_flag = ((position - lag_index >= 0) & (block_mask[0, lag_index - 1] == 1)).astype(
            jnp.float32
        )
        query_term, key_term, value_term = block_terms(moving_keys, moving_values, live_flag)
        grad_query = grad_query + query_term
        carried_keys, carried_values = passed_along((carried_keys, carried_values), "ctx", 1)
        carried_keys = carried_keys + key_term
        carried_values = carried_values + value_term
    home_keys, home_values = (
        passed_along(carried_keys.astype(jnp.bfloat16), "ctx", -(WIN - 1)).astype(
            carried_keys.dtype
        ),
        passed_along(carried_values.astype(jnp.bfloat16), "ctx", -(WIN - 1)).astype(
            carried_values.dtype
        ),
    )
    grad_queries = grad_query.reshape(tokens_here, -1).astype(jnp.bfloat16)
    grad_keys = home_keys.reshape(tokens_here, -1).astype(jnp.bfloat16)
    grad_values = home_values.reshape(tokens_here, -1).astype(jnp.bfloat16)
    received = exchanged(grad_tokens, expert_ids, route_probs)[None]
    grad_weight = jnp.einsum(
        "esf,esd->efd",
        lax.all_gather(hidden_saved, "tp", axis=2, tiled=True),
        received,
        preferred_element_type=jnp.float32,
    ).astype(jnp.bfloat16)
    hidden_sum = lax.psum_scatter(
        jnp.einsum("efd,esd->fes", down_weight, received, preferred_element_type=jnp.float32),
        "tp",
        scatter_dimension=0,
        tiled=True,
    ).transpose(1, 0, 2)
    grad_hidden = hidden_sum.astype(jnp.bfloat16)
    return (grad_queries, grad_keys, grad_values, grad_weight, grad_hidden)


def solution(mesh):
    return jax.shard_map(
        shards,
        mesh=mesh,
        in_specs=(
            P("ctx", "tp"),
            P("ctx", "tp"),
            P("ctx", "tp"),
            P("ctx", "tp"),
            P("ctx", "tp"),
            P("tp", "ctx"),
            P("ctx", None),
            P("ctx", "tp"),
            P("ctx", None),
            P("ctx", None),
            P("ctx", None, "tp"),
            P("ctx", None, "tp"),
        ),
        out_specs=(
            P("ctx", "tp"),
            P("ctx", "tp"),
            P("ctx", "tp"),
            P("ctx", None, "tp"),
            P("ctx", "tp", None),
        ),
        check_vma=False,
    )
```

```python
import jax
import jax.numpy as jnp
from jax import lax
from jax.experimental import pallas as pl
from jax.experimental.pallas import tpu as pltpu
from jax.sharding import PartitionSpec as P

HD = 128
WIN = 4
CTX = 64
CAP = 16
TOK = 256
HEADS = 8
FFT = 384
WIDTH = 1024
SLOTS = CTX * CAP
COL = 8 * CAP
SCALE = HD**-0.5
MESH = pl.DeviceIdType.MESH
F32, BF16 = jnp.float32, jnp.bfloat16


def place(ctx, offset):
    x = lax.rem(ctx // 32 + offset // 32, 2)
    y = lax.rem(lax.rem(ctx // 8, 4) + lax.rem(offset // 8, 4), 4)
    z = lax.rem(lax.rem(ctx, 8) + lax.rem(offset, 8), 8)
    return (x * 4 + y) * 8 + z


def dot(a, b):
    return jnp.dot(a, b, preferred_element_type=F32)


def aligned(index, size):
    return pl.ds(pl.multiple_of(index * size, size), size)


def kernel(
    queries, keys, values, outputs, grad_out, log_sums, block_mask, tokens, ids, probs, hidden, down,
    dq_stack, dkv, gw, gh,
    q_stack, g_stack, o_stack, q_turned, g_turned, log_rows, delta, mask_row, kv, k_turned, p_all, s_all,
    home, ret_out, ret_in,
    tok, id_rows, prob_rows, routed, received, hid, hid_all, down_here, total,
    own_part, far_part, near_out, near_in, far_out, far_in,
    in_sems, kv_sems, ret_sems, hid_sems, send_sem, recv_sems, near_sems, far_sems,
):
    ctx, tp = lax.axis_index("ctx"), lax.axis_index("tp")
    sibling = (tp // 2) * 2 + (1 - lax.rem(tp, 2))
    across = lax.rem(tp + 2, 4)
    diagonal = lax.rem(sibling + 2, 4)
    barrier = pltpu.get_barrier_semaphore()

    def greet(offset, carry):
        pl.semaphore_signal(barrier, inc=1, device_id=(place(ctx, offset), tp), device_id_type=MESH)
        return carry

    lax.fori_loop(1, CTX, greet, 0)
    for other in (sibling, across):
        pl.semaphore_signal(barrier, inc=1, device_id=(ctx, other), device_id_type=MESH)

    def fetch(index, source, target):
        copy = pltpu.make_async_copy(source, target, in_sems.at[index])
        copy.start()
        return copy

    get_ids = fetch(0, ids, id_rows)
    get_probs = fetch(1, probs, prob_rows)
    get_tokens = fetch(2, tokens, tok)
    get_hidden = fetch(3, hidden, hid)
    get_keys = fetch(4, keys, kv.at[0, 0])
    get_values = fetch(5, values, kv.at[0, 1])
    get_logs = fetch(6, log_sums, log_rows)
    get_mask = fetch(7, block_mask, mask_row)
    get_heads = []
    for index, (source, target) in enumerate(((queries, q_stack), (grad_out, g_stack), (outputs, o_stack))):
        for head in range(HEADS):
            get_heads.append(
                fetch(
                    9 + index * HEADS + head,
                    source.at[:, pl.ds(head * HD, HD)],
                    target.at[pl.ds(head * TOK, TOK)],
                )
            )
    get_down = fetch(8, down, down_here)

    get_hidden.wait()

    def turn_hidden(part, carry):
        hid_all[tp, :, aligned(part, 256)] = hid[aligned(part, 256), :].T
        return carry

    lax.fori_loop(0, SLOTS // 256, turn_hidden, 0)

    get_ids.wait()
    get_probs.wait()
    experts = lax.broadcasted_iota(jnp.int32, (CTX, TOK), 0)
    named = [id_rows[rank : rank + 1, :] == experts for rank in range(2)]
    before = (
        lax.broadcasted_iota(jnp.int32, (TOK, TOK), 0) < lax.broadcasted_iota(jnp.int32, (TOK, TOK), 1)
    ).astype(BF16)
    earlier = dot((named[0] | named[1]).astype(BF16), before)
    wanted = []
    for rank in range(2):
        slot = jnp.sum(jnp.where(named[rank], earlier, 0.0), axis=0, keepdims=True).astype(jnp.int32)
        wanted.append(id_rows[rank : rank + 1, :] * CAP + slot)
    get_tokens.wait()

    def pick(column, carry):
        slots = lax.broadcasted_iota(jnp.int32, (COL, TOK), 0) + column * COL
        chosen = [slots == wanted[rank] for rank in range(2)]
        factor = jnp.sum(
            jnp.where(chosen[0], prob_rows[0:1, :], 0.0) + jnp.where(chosen[1], prob_rows[1:2, :], 0.0),
            axis=1,
            keepdims=True,
        )
        rows = dot((chosen[0] | chosen[1]).astype(BF16), tok[...])
        routed[aligned(column, COL), :] = (rows * factor).astype(BF16)
        return carry

    lax.fori_loop(0, 8, pick, 0)
    get_keys.wait()
    get_values.wait()
    pl.semaphore_wait(barrier, CTX + 1)

    def remote(source, target, sends, receives, device):
        copy = pltpu.make_async_remote_copy(
            src_ref=source, dst_ref=target, send_sem=sends, recv_sem=receives, device_id=device, device_id_type=MESH
        )
        copy.start()
        return copy

    kv_copies = [
        remote(
            kv.at[0], kv.at[lag], kv_sems.at[0, lag - 1], kv_sems.at[1, lag - 1], (lax.rem(ctx + lag, CTX), tp)
        )
        for lag in range(1, WIN)
    ]
    hid_across = remote(hid_all.at[tp], hid_all.at[tp], hid_sems.at[0, 0], hid_sems.at[1, 0], (ctx, across))
    hid_near = remote(hid_all.at[tp], hid_all.at[tp], hid_sems.at[0, 1], hid_sems.at[1, 1], (ctx, sibling))

    def send(index, carry):
        column = lax.rem(index // 8, 2) * 4 + index // 16
        target = place(ctx, column * 8 + lax.rem(index, 8))
        remote(
            routed.at[aligned(target, CAP)],
            received.at[aligned(ctx, CAP)],
            send_sem,
            recv_sems.at[column],
            (target, tp),
        )
        return carry

    lax.fori_loop(1, CTX, send, 0)
    received[aligned(ctx, CAP), :] = routed[aligned(ctx, CAP), :]

    for copy in get_heads:
        copy.wait()
    get_logs.wait()
    get_mask.wait()

    def turn_heads(head, carry):
        rows, lanes = aligned(head, TOK), aligned(head, HD)
        q_turned[lanes, :] = q_stack[rows, :].T
        turned = g_stack[rows, :].T
        g_turned[lanes, :] = turned
        delta[pl.ds(head, 1), :] = jnp.sum(
            turned.astype(F32) * o_stack[rows, :].T.astype(F32), axis=0, keepdims=True
        )
        return carry

    lax.fori_loop(0, HEADS, turn_heads, 0)

    def attend(lag, carry):
        @pl.when(lag > 0)
        def _():
            pltpu.make_async_copy(kv.at[lag], kv.at[lag], kv_sems.at[1, lag - 1]).wait()

        lag_rows = aligned(lag, TOK)
        k_turned[:, lag_rows] = kv[lag, 0].T
        given = jnp.sum(
            jnp.where(
                lax.broadcasted_iota(jnp.int32, (1, WIN - 1), 1) == lag - 1, mask_row[...], 0
            ).astype(F32),
            axis=1,
            keepdims=True,
        )
        live = jnp.where(lag == 0, 1.0, jnp.where(ctx - lag >= 0, given, 0.0))
        key_at = lax.broadcasted_iota(jnp.int32, (TOK, TOK), 0)
        query_at = lax.broadcasted_iota(jnp.int32, (TOK, TOK), 1)
        factor = jnp.where(key_at <= query_at + lag * TOK, live, 0.0)

        def head_terms(head, carry):
            lanes = aligned(head, HD)
            scores = dot(kv[lag, 0], q_turned[lanes, :]) * SCALE
            weights = jnp.exp(scores - log_rows[pl.ds(head, 1), :]) * factor
            p_all[:, aligned(head, TOK)] = weights.astype(BF16)
            grads = dot(kv[lag, 1], g_turned[lanes, :])
            s_all[lag_rows, aligned(head, TOK)] = (weights * (grads - delta[pl.ds(head, 1), :])).astype(BF16)
            return carry

        lax.fori_loop(0, HEADS, head_terms, 0)
        key_term = dot(s_all[lag_rows, :], q_stack[...])
        value_term = dot(p_all[...], g_stack[...])

        @pl.when(lag == 0)
        def _():
            home[0] = key_term
            home[1] = value_term

        @pl.when(lag > 0)
        def _():
            ret_out[lag - 1, 0] = key_term.astype(BF16)
            ret_out[lag - 1, 1] = value_term.astype(BF16)
            remote(
                ret_out.at[lag - 1],
                ret_in.at[lag - 1],
                ret_sems.at[0, lag - 1],
                ret_sems.at[1, lag - 1],
                (lax.rem(ctx + CTX - lag, CTX), tp),
            )

        return carry

    lax.fori_loop(0, WIN, attend, 0)

    def finish_queries(head, carry):
        turned = dot(k_turned[...], s_all[:, aligned(head, TOK)]) * SCALE
        dq_stack[aligned(head, TOK), :] = turned.T.astype(BF16)
        return carry

    lax.fori_loop(0, HEADS, finish_queries, 0)
    hid_across.wait()
    hid_on = remote(hid_all.at[across], hid_all.at[across], hid_sems.at[0, 2], hid_sems.at[1, 2], (ctx, sibling))
    get_down.wait()

    def columns_of(pair):
        x, y = ctx // 32, lax.rem(ctx // 8, 4)
        there = lax.rem(y + 4 - pair, 4)
        return x * 4 + there, (1 - x) * 4 + there

    def take(pair):
        for half, column in enumerate((pair, pair + 4)):
            rows = pl.ds(0, COL - CAP) if half == 0 and isinstance(pair, int) and pair == 0 else pl.ds(0, COL)
            pltpu.make_async_copy(received.at[rows], received.at[rows], recv_sems.at[column]).wait()
        a, b = columns_of(pair)
        rows = jnp.concatenate([received[aligned(a, COL), :], received[aligned(b, COL), :]], axis=0)

        def part(owner):
            return lax.dot_general(
                down_here[aligned(owner, FFT), :], rows, (((1,), (1,)), ((), ())), preferred_element_type=F32
            )

        near_out[pair, 0] = part(diagonal).astype(BF16)
        near_out[pair, 1] = part(sibling).astype(BF16)
        remote(near_out.at[pair], near_in.at[pair], near_sems.at[0, pair], near_sems.at[1, pair], (ctx, sibling))
        far_part[...] = part(across)
        own_part[pair] = part(tp)

    def weigh(pair, first, last, final):
        a, b = columns_of(pair)

        def tile(index, carry):
            owner, inner = index // 3, lax.rem(index, 3)
            left = jnp.concatenate(
                [
                    hid_all[owner, aligned(inner, 128), aligned(a, COL)],
                    hid_all[owner, aligned(inner, 128), aligned(b, COL)],
                ],
                axis=1,
            )
            right = jnp.concatenate([received[aligned(a, COL), :], received[aligned(b, COL), :]], axis=0)
            here = aligned(index, 128)
            term = dot(left, right)
            if final:
                gw[here, :] = (total[here, :] + term).astype(BF16)
            elif isinstance(pair, int):
                total[here, :] = term
            else:
                total[here, :] = total[here, :] + term
            return carry

        lax.fori_loop(first, last, tile, 0)

    def pass_on(pair):
        pltpu.make_async_copy(near_in.at[pair], near_in.at[pair], near_sems.at[1, pair]).wait()
        far_out[pair] = (far_part[...] + near_in[pair, 0].astype(F32)).astype(BF16)
        remote(far_out.at[pair], far_in.at[pair], far_sems.at[0, pair], far_sems.at[1, pair], (ctx, across))

    def settle(pair):
        pltpu.make_async_copy(far_in.at[pair], far_in.at[pair], far_sems.at[1, pair]).wait()
        done = (own_part[pair] + near_in[pair, 1].astype(F32) + far_in[pair].astype(F32)).astype(BF16)
        a, b = columns_of(pair)
        gh[:, aligned(a, COL)] = done[:, :COL]
        gh[:, aligned(b, COL)] = done[:, COL:]

    last = 3
    take(0)
    hid_near.wait()
    hid_on.wait()
    weigh(0, 0, 12, False)
    pass_on(0)

    def middle(pair, carry):
        take(pair)
        weigh(pair, 0, 12, False)
        pass_on(pair)
        settle(pair - 1)
        return carry

    lax.fori_loop(1, last, middle, 0)

    for lag in range(1, WIN):
        pltpu.make_async_copy(ret_in.at[lag - 1], ret_in.at[lag - 1], ret_sems.at[1, lag - 1]).wait()
    for index in range(2):
        whole = home[index]
        for lag in range(1, WIN):
            whole = whole + ret_in[lag - 1, index].astype(F32)
        dkv[index] = (whole * (SCALE if index == 0 else 1.0)).astype(BF16)

    take(last)
    weigh(last, 0, 6, True)
    pass_on(last)
    weigh(last, 6, 12, True)
    settle(last - 1)
    settle(last)

    for copy in kv_copies:
        copy.wait_send()
    for lag in range(1, WIN):
        pltpu.make_async_copy(ret_out.at[lag - 1], ret_out.at[lag - 1], ret_sems.at[0, lag - 1]).wait()
    for pair in range(4):
        pltpu.make_async_copy(near_out.at[pair], near_out.at[pair], near_sems.at[0, pair]).wait()
        pltpu.make_async_copy(far_out.at[pair], far_out.at[pair], far_sems.at[0, pair]).wait()
    rows = pl.ds(0, (CTX - 1) * CAP)
    pltpu.make_async_copy(routed.at[rows], routed.at[rows], send_sem).wait()


def hand_over(dq_stack, dkv, gw, gh, grad_queries, grad_keys, grad_values, grad_weight, grad_hidden, sems):
    pairs = [
        (dq_stack.at[pl.ds(head * TOK, TOK)], grad_queries.at[:, pl.ds(head * HD, HD)]) for head in range(HEADS)
    ]
    pairs += [(dkv.at[0], grad_keys), (dkv.at[1], grad_values), (gh, grad_hidden)]
    pairs += [(gw.at[pl.ds(part * FFT, FFT)], grad_weight.at[pl.ds(part * FFT, FFT)]) for part in range(4)]
    copies = [pltpu.make_async_copy(*pair, sems.at[index]) for index, pair in enumerate(pairs)]
    for copy in copies:
        copy.start()
    for copy in copies:
        copy.wait()


def shards(
    queries,
    keys,
    values,
    outputs,
    grad_out,
    log_sums,
    block_mask,
    grad_tokens,
    expert_ids,
    route_probs,
    hidden_saved,
    down_weight,
):
    hbm = pl.BlockSpec(memory_space=pltpu.HBM)
    vmem = pltpu.VMEM
    dma = pltpu.SemaphoreType.DMA
    heads = (HEADS * TOK, HD)
    turned = (HEADS * HD, TOK)
    results = pl.pallas_call(
        kernel,
        out_shape=[
            vmem(heads, BF16),
            vmem((2, TOK, HD), BF16),
            vmem((4 * FFT, WIDTH), BF16),
            vmem((FFT, SLOTS), BF16),
        ],
        in_specs=[hbm] * 12,
        out_specs=[pl.BlockSpec(memory_space=vmem)] * 4,
        scratch_shapes=[
            vmem(heads, BF16),
            vmem(heads, BF16),
            vmem(heads, BF16),
            vmem(turned, BF16),
            vmem(turned, BF16),
            vmem((HEADS, TOK), F32),
            vmem((HEADS, TOK), F32),
            vmem((1, WIN - 1), jnp.int32),
            vmem((WIN, 2, TOK, HD), BF16),
            vmem((HD, WIN * TOK), BF16),
            vmem((TOK, HEADS * TOK), BF16),
            vmem((WIN * TOK, HEADS * TOK), BF16),
            vmem((2, TOK, HD), F32),
            vmem((WIN - 1, 2, TOK, HD), BF16),
            vmem((WIN - 1, 2, TOK, HD), BF16),
            vmem((TOK, WIDTH), BF16),
            vmem((2, TOK), jnp.int32),
            vmem((2, TOK), F32),
            vmem((SLOTS, WIDTH), BF16),
            vmem((SLOTS, WIDTH), BF16),
            vmem((SLOTS, FFT), BF16),
            vmem((4, FFT, SLOTS), BF16),
            vmem((4 * FFT, WIDTH), BF16),
            vmem((4 * FFT, WIDTH), F32),
            vmem((4, FFT, 2 * COL), F32),
            vmem((FFT, 2 * COL), F32),
            vmem((4, 2, FFT, 2 * COL), BF16),
            vmem((4, 2, FFT, 2 * COL), BF16),
            vmem((4, FFT, 2 * COL), BF16),
            vmem((4, FFT, 2 * COL), BF16),
            dma((9 + 3 * HEADS,)),
            dma((2, WIN - 1)),
            dma((2, WIN - 1)),
            dma((2, 3)),
            dma,
            dma((8,)),
            dma((2, 4)),
            dma((2, 4)),
        ],
        compiler_params=pltpu.CompilerParams(
            collective_id=0, has_side_effects=True, vmem_limit_bytes=48 * 2**20
        ),
        name="layer",
    )(
        *[
            pltpu.with_memory_space_constraint(array, pltpu.HBM)
            for array in (
                queries,
                keys,
                values,
                outputs,
                grad_out,
                log_sums,
                block_mask,
                grad_tokens,
                expert_ids.T,
                route_probs.T,
                hidden_saved[0],
                down_weight[0],
            )
        ]
    )
    grad_queries, grad_keys, grad_values, grad_weight, grad_hidden = pl.pallas_call(
        hand_over,
        out_shape=[
            jax.ShapeDtypeStruct((TOK, WIDTH), BF16),
            jax.ShapeDtypeStruct((TOK, HD), BF16),
            jax.ShapeDtypeStruct((TOK, HD), BF16),
            jax.ShapeDtypeStruct((4 * FFT, WIDTH), BF16),
            jax.ShapeDtypeStruct((FFT, SLOTS), BF16),
        ],
        in_specs=[pl.BlockSpec(memory_space=vmem)] * 4,
        out_specs=[hbm] * 5,
        scratch_shapes=[dma((HEADS + 7,))],
        compiler_params=pltpu.CompilerParams(vmem_limit_bytes=8 * 2**20),
        name="results",
    )(*[pltpu.with_memory_space_constraint(result, pltpu.VMEM) for result in results])
    return grad_queries, grad_keys, grad_values, grad_weight[None], grad_hidden[None]


def solution(mesh):
    return jax.shard_map(
        shards,
        mesh=mesh,
        in_specs=(
            P("ctx", "tp"),
            P("ctx", "tp"),
            P("ctx", "tp"),
            P("ctx", "tp"),
            P("ctx", "tp"),
            P("tp", "ctx"),
            P("ctx", None),
            P("ctx", "tp"),
            P("ctx", None),
            P("ctx", None),
            P("ctx", None, "tp"),
            P("ctx", None, "tp"),
        ),
        out_specs=(
            P("ctx", "tp"),
            P("ctx", "tp"),
            P("ctx", "tp"),
            P("ctx", None, "tp"),
            P("ctx", "tp", None),
        ),
        check_vma=False,
    )
```

```python
import jax
import jax.numpy as jnp
from jax import lax
from jax.experimental import pallas as pl
from jax.experimental.pallas import tpu as pltpu
from jax.sharding import PartitionSpec as P

HD = 128
WIN = 4
CTX = 64
CAP = 16
TOK = 256
HEADS = 8
FFT = 384
WIDTH = 1024
SLOTS = CTX * CAP
COL = 8 * CAP
SCALE = HD**-0.5
MESH = pl.DeviceIdType.MESH
F32, BF16 = jnp.float32, jnp.bfloat16


def place(ctx, offset):
    x = lax.rem(ctx // 32 + offset // 32, 2)
    y = lax.rem(lax.rem(ctx // 8, 4) + lax.rem(offset // 8, 4), 4)
    z = lax.rem(lax.rem(ctx, 8) + lax.rem(offset, 8), 8)
    return (x * 4 + y) * 8 + z


def dot(a, b):
    return jnp.dot(a, b, preferred_element_type=F32)


def aligned(index, size):
    return pl.ds(pl.multiple_of(index * size, size), size)


def kernel(
    queries, keys, values, outputs, grad_out, log_sums, block_mask, tokens, ids, probs, hidden, down,
    dq_stack, dkv, gw, gh,
    q_stack, g_stack, o_stack, q_turned, g_turned, log_rows, delta, mask_row, kv, k_turned, p_all, s_all,
    home, ret_out, ret_in,
    tok, id_rows, prob_rows, routed, received, hid, hid_all, down_here, total,
    own_part, far_part, near_out, near_in, far_out, far_in,
    in_sems, kv_sems, ret_sems, hid_sems, send_sem, recv_sems, near_sems, far_sems,
):
    ctx, tp = lax.axis_index("ctx"), lax.axis_index("tp")
    sibling = (tp // 2) * 2 + (1 - lax.rem(tp, 2))
    across = lax.rem(tp + 2, 4)
    diagonal = lax.rem(sibling + 2, 4)
    barrier = pltpu.get_barrier_semaphore()

    def greet(offset, carry):
        pl.semaphore_signal(barrier, inc=1, device_id=(place(ctx, offset), tp), device_id_type=MESH)
        return carry

    lax.fori_loop(1, CTX, greet, 0)
    for other in (sibling, across):
        pl.semaphore_signal(barrier, inc=1, device_id=(ctx, other), device_id_type=MESH)

    def fetch(index, source, target):
        copy = pltpu.make_async_copy(source, target, in_sems.at[index])
        copy.start()
        return copy

    get_ids = fetch(0, ids, id_rows)
    get_probs = fetch(1, probs, prob_rows)
    get_tokens = fetch(2, tokens, tok)
    get_hidden = fetch(3, hidden, hid)
    get_keys = fetch(4, keys, kv.at[0, 0])
    get_values = fetch(5, values, kv.at[0, 1])
    get_logs = fetch(6, log_sums, log_rows)
    get_mask = fetch(7, block_mask, mask_row)
    get_heads = []
    for index, (source, target) in enumerate(((queries, q_stack), (grad_out, g_stack), (outputs, o_stack))):
        for head in range(HEADS):
            get_heads.append(
                fetch(
                    9 + index * HEADS + head,
                    source.at[:, pl.ds(head * HD, HD)],
                    target.at[pl.ds(head * TOK, TOK)],
                )
            )
    get_down = fetch(8, down, down_here)

    get_ids.wait()
    get_probs.wait()
    experts = lax.broadcasted_iota(jnp.int32, (CTX, TOK), 0)
    named = [id_rows[rank : rank + 1, :] == experts for rank in range(2)]
    before = (
        lax.broadcasted_iota(jnp.int32, (TOK, TOK), 0) < lax.broadcasted_iota(jnp.int32, (TOK, TOK), 1)
    ).astype(BF16)
    earlier = dot((named[0] | named[1]).astype(BF16), before)
    wanted = []
    for rank in range(2):
        slot = jnp.sum(jnp.where(named[rank], earlier, 0.0), axis=0, keepdims=True).astype(jnp.int32)
        wanted.append(id_rows[rank : rank + 1, :] * CAP + slot)
    get_tokens.wait()

    def pick(column, carry):
        slots = lax.broadcasted_iota(jnp.int32, (COL, TOK), 0) + column * COL
        chosen = [slots == wanted[rank] for rank in range(2)]
        factor = jnp.sum(
            jnp.where(chosen[0], prob_rows[0:1, :], 0.0) + jnp.where(chosen[1], prob_rows[1:2, :], 0.0),
            axis=1,
            keepdims=True,
        )
        rows = dot((chosen[0] | chosen[1]).astype(BF16), tok[...])
        routed[aligned(column, COL), :] = (rows * factor).astype(BF16)
        return carry

    lax.fori_loop(0, 8, pick, 0)
    get_keys.wait()
    get_values.wait()
    pl.semaphore_wait(barrier, CTX + 1)

    def remote(source, target, sends, receives, device):
        copy = pltpu.make_async_remote_copy(
            src_ref=source, dst_ref=target, send_sem=sends, recv_sem=receives, device_id=device, device_id_type=MESH
        )
        copy.start()
        return copy

    kv_copies = [
        remote(
            kv.at[0], kv.at[lag], kv_sems.at[0, lag - 1], kv_sems.at[1, lag - 1], (lax.rem(ctx + lag, CTX), tp)
        )
        for lag in range(1, WIN)
    ]
    def send(index, carry):
        column = lax.rem(index // 8, 2) * 4 + index // 16
        target = place(ctx, column * 8 + lax.rem(index, 8))
        remote(
            routed.at[aligned(target, CAP)],
            received.at[aligned(ctx, CAP)],
            send_sem,
            recv_sems.at[column],
            (target, tp),
        )
        return carry

    lax.fori_loop(1, CTX, send, 0)
    received[aligned(ctx, CAP), :] = routed[aligned(ctx, CAP), :]

    get_hidden.wait()

    def turn_hidden(part, carry):
        hid_all[tp, :, aligned(part, 256)] = hid[aligned(part, 256), :].T
        return carry

    lax.fori_loop(0, SLOTS // 256, turn_hidden, 0)

    hid_across = remote(hid_all.at[tp], hid_all.at[tp], hid_sems.at[0, 0], hid_sems.at[1, 0], (ctx, across))
    hid_near = remote(hid_all.at[tp], hid_all.at[tp], hid_sems.at[0, 1], hid_sems.at[1, 1], (ctx, sibling))

    for copy in get_heads:
        copy.wait()
    get_logs.wait()
    get_mask.wait()

    def turn_heads(head, carry):
        rows, lanes = aligned(head, TOK), aligned(head, HD)
        q_turned[lanes, :] = q_stack[rows, :].T
        turned = g_stack[rows, :].T
        g_turned[lanes, :] = turned
        delta[pl.ds(head, 1), :] = jnp.sum(
            turned.astype(F32) * o_stack[rows, :].T.astype(F32), axis=0, keepdims=True
        )
        return carry

    lax.fori_loop(0, HEADS, turn_heads, 0)

    def attend(lag, carry):
        @pl.when(lag > 0)
        def _():
            pltpu.make_async_copy(kv.at[lag], kv.at[lag], kv_sems.at[1, lag - 1]).wait()

        lag_rows = aligned(lag, TOK)
        k_turned[:, lag_rows] = kv[lag, 0].T
        given = jnp.sum(
            jnp.where(
                lax.broadcasted_iota(jnp.int32, (1, WIN - 1), 1) == lag - 1, mask_row[...], 0
            ).astype(F32),
            axis=1,
            keepdims=True,
        )
        live = jnp.where(lag == 0, 1.0, jnp.where(ctx - lag >= 0, given, 0.0))
        key_at = lax.broadcasted_iota(jnp.int32, (TOK, TOK), 0)
        query_at = lax.broadcasted_iota(jnp.int32, (TOK, TOK), 1)
        factor = jnp.where(key_at <= query_at + lag * TOK, live, 0.0)

        def head_terms(head, carry):
            lanes = aligned(head, HD)
            scores = dot(kv[lag, 0], q_turned[lanes, :]) * SCALE
            weights = jnp.exp(scores - log_rows[pl.ds(head, 1), :]) * factor
            p_all[:, aligned(head, TOK)] = weights.astype(BF16)
            grads = dot(kv[lag, 1], g_turned[lanes, :])
            s_all[lag_rows, aligned(head, TOK)] = (weights * (grads - delta[pl.ds(head, 1), :])).astype(BF16)
            return carry

        lax.fori_loop(0, HEADS, head_terms, 0)
        key_term = dot(s_all[lag_rows, :], q_stack[...])
        value_term = dot(p_all[...], g_stack[...])

        @pl.when(lag == 0)
        def _():
            home[0] = key_term
            home[1] = value_term

        @pl.when(lag > 0)
        def _():
            ret_out[lag - 1, 0] = key_term.astype(BF16)
            ret_out[lag - 1, 1] = value_term.astype(BF16)
            remote(
                ret_out.at[lag - 1],
                ret_in.at[lag - 1],
                ret_sems.at[0, lag - 1],
                ret_sems.at[1, lag - 1],
                (lax.rem(ctx + CTX - lag, CTX), tp),
            )

        return carry

    lax.fori_loop(0, WIN, attend, 0)

    def finish_queries(head, carry):
        turned = dot(k_turned[...], s_all[:, aligned(head, TOK)]) * SCALE
        dq_stack[aligned(head, TOK), :] = turned.T.astype(BF16)
        return carry

    lax.fori_loop(0, HEADS, finish_queries, 0)
    hid_across.wait()
    hid_on = remote(hid_all.at[across], hid_all.at[across], hid_sems.at[0, 2], hid_sems.at[1, 2], (ctx, sibling))
    get_down.wait()

    def columns_of(pair):
        x, y = ctx // 32, lax.rem(ctx // 8, 4)
        there = lax.rem(y + 4 - pair, 4)
        return x * 4 + there, (1 - x) * 4 + there

    def take(pair):
        for half, column in enumerate((pair, pair + 4)):
            rows = pl.ds(0, COL - CAP) if half == 0 and isinstance(pair, int) and pair == 0 else pl.ds(0, COL)
            pltpu.make_async_copy(received.at[rows], received.at[rows], recv_sems.at[column]).wait()
        a, b = columns_of(pair)
        rows = jnp.concatenate([received[aligned(a, COL), :], received[aligned(b, COL), :]], axis=0)

        def part(owner):
            return lax.dot_general(
                down_here[aligned(owner, FFT), :], rows, (((1,), (1,)), ((), ())), preferred_element_type=F32
            )

        near_out[pair, 0] = part(diagonal).astype(BF16)
        near_out[pair, 1] = part(sibling).astype(BF16)
        remote(near_out.at[pair], near_in.at[pair], near_sems.at[0, pair], near_sems.at[1, pair], (ctx, sibling))
        far_part[...] = part(across)
        own_part[pair] = part(tp)

    def weigh(pair, first, last, final):
        a, b = columns_of(pair)

        def tile(index, carry):
            owner, inner = index // 3, lax.rem(index, 3)
            left = jnp.concatenate(
                [
                    hid_all[owner, aligned(inner, 128), aligned(a, COL)],
                    hid_all[owner, aligned(inner, 128), aligned(b, COL)],
                ],
                axis=1,
            )
            right = jnp.concatenate([received[aligned(a, COL), :], received[aligned(b, COL), :]], axis=0)
            here = aligned(index, 128)
            term = dot(left, right)
            if final:
                gw[here, :] = (total[here, :] + term).astype(BF16)
            elif isinstance(pair, int):
                total[here, :] = term
            else:
                total[here, :] = total[here, :] + term
            return carry

        lax.fori_loop(first, last, tile, 0)

    def pass_on(pair):
        pltpu.make_async_copy(near_in.at[pair], near_in.at[pair], near_sems.at[1, pair]).wait()
        far_out[pair] = (far_part[...] + near_in[pair, 0].astype(F32)).astype(BF16)
        remote(far_out.at[pair], far_in.at[pair], far_sems.at[0, pair], far_sems.at[1, pair], (ctx, across))

    def settle(pair):
        pltpu.make_async_copy(far_in.at[pair], far_in.at[pair], far_sems.at[1, pair]).wait()
        done = (own_part[pair] + near_in[pair, 1].astype(F32) + far_in[pair].astype(F32)).astype(BF16)
        a, b = columns_of(pair)
        gh[:, aligned(a, COL)] = done[:, :COL]
        gh[:, aligned(b, COL)] = done[:, COL:]

    last = 3
    take(0)
    hid_near.wait()
    hid_on.wait()
    weigh(0, 0, 12, False)
    pass_on(0)

    def middle(pair, carry):
        take(pair)
        weigh(pair, 0, 12, False)
        pass_on(pair)
        settle(pair - 1)
        return carry

    lax.fori_loop(1, last, middle, 0)

    take(last)
    weigh(last, 0, 6, True)
    pass_on(last)
    weigh(last, 6, 12, True)
    settle(last - 1)
    settle(last)
    for lag in range(1, WIN):
        pltpu.make_async_copy(ret_in.at[lag - 1], ret_in.at[lag - 1], ret_sems.at[1, lag - 1]).wait()
    for index in range(2):
        whole = home[index]
        for lag in range(1, WIN):
            whole = whole + ret_in[lag - 1, index].astype(F32)
        dkv[index] = (whole * (SCALE if index == 0 else 1.0)).astype(BF16)


    for copy in kv_copies:
        copy.wait_send()
    for lag in range(1, WIN):
        pltpu.make_async_copy(ret_out.at[lag - 1], ret_out.at[lag - 1], ret_sems.at[0, lag - 1]).wait()
    for pair in range(4):
        pltpu.make_async_copy(near_out.at[pair], near_out.at[pair], near_sems.at[0, pair]).wait()
        pltpu.make_async_copy(far_out.at[pair], far_out.at[pair], far_sems.at[0, pair]).wait()
    rows = pl.ds(0, (CTX - 1) * CAP)
    pltpu.make_async_copy(routed.at[rows], routed.at[rows], send_sem).wait()


def hand_over(dq_stack, dkv, gw, gh, grad_queries, grad_keys, grad_values, grad_weight, grad_hidden, sems):
    pairs = [
        (dq_stack.at[pl.ds(head * TOK, TOK)], grad_queries.at[:, pl.ds(head * HD, HD)]) for head in range(HEADS)
    ]
    pairs += [(dkv.at[0], grad_keys), (dkv.at[1], grad_values), (gh, grad_hidden)]
    pairs += [(gw.at[pl.ds(part * FFT, FFT)], grad_weight.at[pl.ds(part * FFT, FFT)]) for part in range(4)]
    copies = [pltpu.make_async_copy(*pair, sems.at[index]) for index, pair in enumerate(pairs)]
    for copy in copies:
        copy.start()
    for copy in copies:
        copy.wait()


def shards(
    queries,
    keys,
    values,
    outputs,
    grad_out,
    log_sums,
    block_mask,
    grad_tokens,
    expert_ids,
    route_probs,
    hidden_saved,
    down_weight,
):
    hbm = pl.BlockSpec(memory_space=pltpu.HBM)
    vmem = pltpu.VMEM
    dma = pltpu.SemaphoreType.DMA
    heads = (HEADS * TOK, HD)
    turned = (HEADS * HD, TOK)
    results = pl.pallas_call(
        kernel,
        out_shape=[
            vmem(heads, BF16),
            vmem((2, TOK, HD), BF16),
            vmem((4 * FFT, WIDTH), BF16),
            vmem((FFT, SLOTS), BF16),
        ],
        in_specs=[hbm] * 12,
        out_specs=[pl.BlockSpec(memory_space=vmem)] * 4,
        scratch_shapes=[
            vmem(heads, BF16),
            vmem(heads, BF16),
            vmem(heads, BF16),
            vmem(turned, BF16),
            vmem(turned, BF16),
            vmem((HEADS, TOK), F32),
            vmem((HEADS, TOK), F32),
            vmem((1, WIN - 1), jnp.int32),
            vmem((WIN, 2, TOK, HD), BF16),
            vmem((HD, WIN * TOK), BF16),
            vmem((TOK, HEADS * TOK), BF16),
            vmem((WIN * TOK, HEADS * TOK), BF16),
            vmem((2, TOK, HD), F32),
            vmem((WIN - 1, 2, TOK, HD), BF16),
            vmem((WIN - 1, 2, TOK, HD), BF16),
            vmem((TOK, WIDTH), BF16),
            vmem((2, TOK), jnp.int32),
            vmem((2, TOK), F32),
            vmem((SLOTS, WIDTH), BF16),
            vmem((SLOTS, WIDTH), BF16),
            vmem((SLOTS, FFT), BF16),
            vmem((4, FFT, SLOTS), BF16),
            vmem((4 * FFT, WIDTH), BF16),
            vmem((4 * FFT, WIDTH), F32),
            vmem((4, FFT, 2 * COL), F32),
            vmem((FFT, 2 * COL), F32),
            vmem((4, 2, FFT, 2 * COL), BF16),
            vmem((4, 2, FFT, 2 * COL), BF16),
            vmem((4, FFT, 2 * COL), BF16),
            vmem((4, FFT, 2 * COL), BF16),
            dma((9 + 3 * HEADS,)),
            dma((2, WIN - 1)),
            dma((2, WIN - 1)),
            dma((2, 3)),
            dma,
            dma((8,)),
            dma((2, 4)),
            dma((2, 4)),
        ],
        compiler_params=pltpu.CompilerParams(
            collective_id=0, has_side_effects=True, vmem_limit_bytes=48 * 2**20
        ),
        name="layer",
    )(
        *[
            pltpu.with_memory_space_constraint(array, pltpu.HBM)
            for array in (
                queries,
                keys,
                values,
                outputs,
                grad_out,
                log_sums,
                block_mask,
                grad_tokens,
                expert_ids.T,
                route_probs.T,
                hidden_saved[0],
                down_weight[0],
            )
        ]
    )
    grad_queries, grad_keys, grad_values, grad_weight, grad_hidden = pl.pallas_call(
        hand_over,
        out_shape=[
            jax.ShapeDtypeStruct((TOK, WIDTH), BF16),
            jax.ShapeDtypeStruct((TOK, HD), BF16),
            jax.ShapeDtypeStruct((TOK, HD), BF16),
            jax.ShapeDtypeStruct((4 * FFT, WIDTH), BF16),
            jax.ShapeDtypeStruct((FFT, SLOTS), BF16),
        ],
        in_specs=[pl.BlockSpec(memory_space=vmem)] * 4,
        out_specs=[hbm] * 5,
        scratch_shapes=[dma((HEADS + 7,))],
        compiler_params=pltpu.CompilerParams(vmem_limit_bytes=8 * 2**20),
        name="results",
    )(*[pltpu.with_memory_space_constraint(result, pltpu.VMEM) for result in results])
    return grad_queries, grad_keys, grad_values, grad_weight[None], grad_hidden[None]


def solution(mesh):
    return jax.shard_map(
        shards,
        mesh=mesh,
        in_specs=(
            P("ctx", "tp"),
            P("ctx", "tp"),
            P("ctx", "tp"),
            P("ctx", "tp"),
            P("ctx", "tp"),
            P("tp", "ctx"),
            P("ctx", None),
            P("ctx", "tp"),
            P("ctx", None),
            P("ctx", None),
            P("ctx", None, "tp"),
            P("ctx", None, "tp"),
        ),
        out_specs=(
            P("ctx", "tp"),
            P("ctx", "tp"),
            P("ctx", "tp"),
            P("ctx", None, "tp"),
            P("ctx", "tp", None),
        ),
        check_vma=False,
    )
```
